512 devices in a mesh: row: 16 (over z), col: 32 (over x, y, core).
Axes of the slice: x: 4, y: 4, z: 16, core: 2. Of those that a mesh axis runs over, the one named last changes fastest.
Arguments:
- trail_adj: float32 [16, 768, 12288], P(None, 'col', 'row'), as said below
- trail_factor: float32 [12288, 768], P(('row', 'col')), may hold values from -0.0546875 to 0.0546875
- trail_lbar: float32 [12288, 768], P(('row', 'col')), may hold values from -6 to 6
- head_factor: float32 [6, 65536], P(None, ('row', 'col')), as said below
- head_inverse: float32 [3, 65536], P(None, ('row', 'col')), as said below
- head_lbar: float32 [6, 65536], P(None, ('row', 'col')), may hold values from -6 to 6
Outputs:
- trail_cols: float32 [12288, 768], P(('row', 'col'))
- head_adj: float32 [6, 65536], P(None, ('row', 'col'))
The draws below stay inside these ranges and needn't reach their ends.
Inputs may be any that keep to these rules, and one draw needn't show every extreme that they name: trail_adj read as the matrix Z is exactly symmetric. The diagonal blocks F[k, k] of head_factor are lower triangular with a positive diagonal. Block k of head_inverse is lower triangular and is the inverse of F[k, k] up to float32 rounding.
All inputs are finite; a program needn't handle non-finite values.
Results may differ from the reference program's by a relative error of at most 0.00026.
Values sent between devices are 32-bit elements; how exact they have to be, the bound alone decides.
A program may use at most 64 MiB of HBM per device.

```python
import math
import jax
import jax.numpy as jnp
from jax import lax

NB = 256
NT = 12288
N_ROW = 16


def head_pair(key):
    folded = jax.random.fold_in(key, 4051)
    subkeys = jax.random.split(folded, 3)
    diagonal = jax.random.uniform(subkeys[0], (3, NB), jnp.float32, 1.0, 2.0)
    strict_lower = jnp.tril(jax.random.normal(subkeys[1], (3, NB, NB), jnp.float32), -1) * (0.45 / math.sqrt(NB))
    diag_blocks = strict_lower + diagonal[:, :, None] * jnp.eye(NB, dtype=jnp.float32)[None, :, :]
    off_blocks = jax.random.normal(subkeys[2], (3, NB, NB), jnp.float32) / math.sqrt(NB)
    inverse = jnp.tril(jnp.linalg.inv(diag_blocks))
    factor = jnp.stack([diag_blocks[0], off_blocks[0], diag_blocks[1], off_blocks[1], off_blocks[2], diag_blocks[2]])
    return (factor.reshape(6, NB * NB), inverse.reshape(3, NB * NB))


def draw_head_factor(key, part):
    return head_pair(key)[0]


def draw_head_inverse(key, part):
    return head_pair(key)[1]


def draw_trail_adj(key, part):
    folded = jax.random.fold_in(key, 811)
    raw_values = jax.random.normal(folded, (NT, NT), jnp.float32)
    symmetric = (raw_values + raw_values.T) * 0.70710677
    return symmetric.reshape(N_ROW, NT // N_ROW, NT)


def block_levels(stream_key, dims, cuts, low, largest):
    level = 1.0
    for position, shards_of in cuts:
        heights = jax.random.uniform(jax.random.fold_in(jax.random.fold_in(stream_key, 6), position), (shards_of,), jnp.float32, low / len(cuts), largest / len(cuts))
        level = level * jnp.repeat(jnp.exp(heights), dims[position] // shards_of).reshape((-1,) + (1,) * (len(dims) - 1 - position))
    return level


def centred(own_key, extent, spread, limit, shards=(), held_as=jnp.bfloat16):
    drawn = spread * jax.random.normal(own_key, extent, jnp.float32)
    if shards:
        drawn = drawn * block_levels(own_key, extent, shards, -0.22, 0.18)
    return jnp.clip(drawn, -limit, limit).astype(held_as)


def setup_inputs(seed: int = 0) -> dict:
    splits = jax.random.split(jax.random.key(seed), 7)
    trail_adj = draw_trail_adj(jax.random.fold_in(splits[6], 71), 0)
    trail_factor = centred(splits[1], (NT, 3 * NB), NT ** -0.5, 0.0546875, ((0, 512),), jnp.float32)
    trail_lbar = centred(splits[2], (NT, 3 * NB), 1.0, 6.0, ((0, 512),), jnp.float32)
    head_factor = draw_head_factor(jax.random.fold_in(splits[6], 71), 0)
    head_inverse = draw_head_inverse(jax.random.fold_in(splits[6], 71), 0)
    head_lbar = centred(splits[5], (6, NB * NB), 1.0, 6.0, ((1, 512),), jnp.float32)
    return {"trail_adj": trail_adj, "trail_factor": trail_factor, "trail_lbar": trail_lbar, "head_factor": head_factor, "head_inverse": head_inverse, "head_lbar": head_lbar}


highest = lax.Precision.HIGHEST

def matmul(left, right):
    return jnp.dot(left.astype(jnp.float32), right.astype(jnp.float32), precision=highest, preferred_element_type=jnp.float32)

def contract_rows(left, right):
    return lax.dot_general(left.astype(jnp.float32), right.astype(jnp.float32), (((0,), (0,)), ((), ())), precision=highest, preferred_element_type=jnp.float32)

def pair_index(target, source):
    return target * (target + 1) // 2 + source

def halve_lower(matrix):
    return jnp.tril(matrix) - 0.5 * jnp.diag(jnp.diag(matrix))

def chol_adjoint(factor, inverse, totals):
    inner = halve_lower(matmul(factor.T, totals))
    mapped = matmul(matmul(inverse.T, inner), inverse)
    return 0.5 * (mapped + mapped.T)

def trail_column(column, product, lbar_rows, columns, factor_blocks, inverse_blocks, breadth):
    gradient = lbar_rows[:, column * breadth:(column + 1) * breadth] - 2.0 * product[:, column * breadth:(column + 1) * breadth]
    for source in range(column + 1, 3):
        gradient = gradient - 2.0 * matmul(columns[source], factor_blocks[pair_index(source, column)])
    return 0.5 * matmul(gradient, inverse_blocks[column])

def trail_terms_of(column, columns, factor_rows, breadth):
    own_rows = factor_rows[:, column * breadth:(column + 1) * breadth]
    terms = [contract_rows(2.0 * columns[column], own_rows)]
    for target in range(column + 1, 3):
        terms.append(contract_rows(columns[target], own_rows))
    return terms

def head_step(column, blocks, factor_blocks, inverse_blocks, lbar_blocks, sums):
    totals = lbar_blocks[pair_index(column, column)] - sums[0]
    for target in range(column + 1, 3):
        summed = sums[target - column]
        for source in range(column + 1, 3):
            if target >= source:
                mirror = blocks[pair_index(target, source)]
            else:
                mirror = blocks[pair_index(source, target)].T
            summed = summed + matmul(mirror, factor_blocks[pair_index(source, column)])
        carried = matmul(lbar_blocks[pair_index(target, column)] - 2.0 * summed, inverse_blocks[column])
        blocks[pair_index(target, column)] = 0.5 * carried
        totals = totals - contract_rows(carried, factor_blocks[pair_index(target, column)])
    blocks[pair_index(column, column)] = chol_adjoint(factor_blocks[pair_index(column, column)], inverse_blocks[column], totals)

def reference(trail_adj, trail_factor, trail_lbar, head_factor, head_inverse, head_lbar):
    adjoint = trail_adj.reshape(NT, NT)
    product = matmul(adjoint, trail_factor)
    factor_blocks = head_factor.reshape(6, NB, NB)
    inverse_blocks = head_inverse.reshape(3, NB, NB)
    lbar_blocks = head_lbar.reshape(6, NB, NB)
    columns = [None, None, None]
    for column in (2, 1, 0):
        columns[column] = trail_column(column, product, trail_lbar, columns, factor_blocks, inverse_blocks, NB)
    blocks = [None, None, None, None, None, None]
    for column in (2, 1, 0):
        sums = jnp.stack(trail_terms_of(column, columns, trail_factor, NB))
        head_step(column, blocks, factor_blocks, inverse_blocks, lbar_blocks, sums)
    return (jnp.concatenate(columns, axis=1), jnp.stack(blocks).reshape(6, NB * NB))
```

```python
import functools

import jax
import jax.numpy as jnp
from jax import lax
from jax.experimental import pallas as pl
from jax.experimental.pallas import tpu as pltpu
from jax.sharding import PartitionSpec as P

MESH = pl.DeviceIdType.MESH
NB = 256
HALF = 128
NZ = 16
NQ = 16
RING = 8
STOP = 99


def dot(left, right):
    return jnp.dot(left, right, precision=lax.Precision.HIGH, preferred_element_type=jnp.float32)


def kernel(
    z_ref, f_ref, b_ref, hf_ref, hi_ref, hl_ref, xt_ref, head_ref,
    zt, fz, y, yr, pr, zslot_f, zslot_i, hx, hm, nat, nrecv, tsum, trecv, zsend, zrecv,
    ring_send, ring_recv, hz_send, hz_recv, hx_send, hx_recv, hs_sem, ys_sem, yx_send, yx_recv,
    xs_sem, xx_send, xx_recv, xz_send, xz_recv,
):
    row = lax.axis_index("row")
    col = lax.axis_index("col")
    core = lax.rem(col, 2)
    chip = col // 2
    other = 1 - core
    sibling = (row, chip * 2 + other)

    def along_row(step):
        return (lax.rem(row + step, NZ), col)

    def along_col(step):
        return (row, lax.rem(chip + step, NQ) * 2 + core)

    def remote(src, dst, send, recv, target):
        return pltpu.make_async_remote_copy(
            src_ref=src, dst_ref=dst, send_sem=send, recv_sem=recv, device_id=target, device_id_type=MESH
        )

    def wait(region, sem):
        pltpu.make_async_copy(region, region, sem).wait()

    barrier = pltpu.get_barrier_semaphore()
    pl.semaphore_signal(barrier, inc=1, device_id=sibling, device_id_type=MESH)

    def greet(step, carry):
        pl.semaphore_signal(barrier, inc=1, device_id=along_row(step), device_id_type=MESH)
        pl.semaphore_signal(barrier, inc=1, device_id=along_col(step), device_id_type=MESH)
        return carry

    lax.fori_loop(1, NZ, greet, 0)
    for panel in range(3):
        fz[panel, row] = f_ref[:, panel * NB : (panel + 1) * NB]
    zslot_f[row] = hf_ref[...]
    zslot_i[row] = hi_ref[...]
    pl.semaphore_wait(barrier, 31)

    right = along_row(1)
    left = along_row(NZ - 1)

    def ring_copy(panel, way, step):
        if way == 0:
            slot, target = lax.rem(row - step + NZ, NZ), right
        else:
            slot, target = lax.rem(row + step, NZ), left
        if step == RING - 1:
            block = fz.at[panel, slot, :, pl.ds(way * HALF, HALF)]
        else:
            block = fz.at[panel, slot]
        return remote(block, block, ring_send, ring_recv.at[way, panel, step], target)

    def ring_landed(panel, way, step):
        if step == RING - 1:
            region = fz.at[panel, 0, :, pl.ds(way * HALF, HALF)]
        else:
            region = fz.at[panel, 0]
        wait(region, ring_recv.at[way, panel, step])

    def ring_step(step):
        for panel in (2, 1, 0):
            for way in (0, 1):
                if step > 0:
                    ring_landed(panel, way, step - 1)
                ring_copy(panel, way, step).start()

    def head_send(step, carry):
        remote(hf_ref, zslot_f.at[row], hz_send, hz_recv.at[0], along_row(step)).start()
        remote(hi_ref, zslot_i.at[row], hz_send, hz_recv.at[1], along_row(step)).start()
        return carry

    def turn(slab):
        rows = z_ref[:, :, slab * HALF : (slab + 1) * HALF].reshape(NZ * 24, HALF)
        hm[slab * HALF : (slab + 1) * HALF, :] = rows.T

    ring_step(0)
    lax.fori_loop(1, NZ, head_send, 0)
    turn(0)
    turn(1)
    ring_step(1)
    turn(2)
    ring_step(2)
    turn(3)
    ring_step(3)
    turn(4)
    wait(zslot_f.at[pl.ds(0, NZ - 1)], hz_recv.at[0])
    wait(zslot_i.at[pl.ds(0, NZ - 1)], hz_recv.at[1])
    for block in range(6):
        hx[core, chip, block] = zslot_f[:, block, :]
    for block in range(3):
        hx[core, chip, 6 + block] = zslot_i[:, block, :]

    def head_spread(step, carry):
        remote(hx.at[core, chip], hx.at[core, chip], hx_send, hx_recv, along_col(step)).start()
        return carry

    lax.fori_loop(1, NQ, head_spread, 0)
    ring_step(4)
    turn(5)
    ring_step(5)
    for half in range(2):
        for part in range(NQ):
            start = (part * 2 + half) * 24
            zt[half, part * 24 : (part + 1) * 24, :] = hm[start : start + 24, :]
    ring_step(6)
    ring_step(7)
    for panel in (2, 1, 0):
        for way in (0, 1):
            ring_landed(panel, way, RING - 1)
    if STOP <= 1:
        xt_ref[...] = fz[0, 0][:, :1] + jnp.zeros_like(xt_ref)
        head_ref[...] = zt[0, :6, :128]

    head = {}
    y_copies, s_copies = {}, {}
    if STOP >= 2:
        for panel in (2, 1, 0):
            factor = fz[panel].reshape(NZ * 24, NB)
            y[panel, other] = dot(zt[other], factor).reshape(NQ, 24, NB)
            y_copies[panel] = remote(y.at[panel, other], yr.at[panel], ys_sem.at[0, panel], ys_sem.at[1, panel], sibling)
            y_copies[panel].start()
            y[panel, core] = dot(zt[core], factor).reshape(NQ, 24, NB)

    if STOP >= 3:
        for panel in (2, 1, 0):
            y_copies[panel].wait_recv()
            y[panel, core] = y[panel, core] + yr[panel]

            def spread(step, carry):
                remote(
                    y.at[panel, core, lax.rem(chip + step, NQ)], pr.at[panel, step - 1],
                    yx_send.at[panel], yx_recv.at[panel], along_col(step),
                ).start()
                return carry

            lax.fori_loop(1, NQ, spread, 0)

    wait(hx.at[0, pl.ds(0, NQ - 1)], hx_recv)
    head_copy = remote(hx.at[core], hx.at[core], hs_sem.at[0], hs_sem.at[1], sibling)
    head_copy.start()
    head_copy.wait_recv()

    blocks = []
    if STOP >= 4:
        for block in range(9):
            for half in range(2):
                rows = hx[half, :, block].reshape(NB, HALF)
                nat[half, block] = rows
            halves = []
            for half in range(2):
                pieces = [nat[half, block, pl.ds(z, NQ, stride=NQ), :] for z in range(NZ)]
                halves.append(jnp.concatenate(pieces, axis=0))
            blocks.append(jnp.concatenate(halves, axis=1))
        f_blocks, w_blocks = blocks[:6], blocks[6:]
        for block in range(6):
            head["f", block] = f_blocks[block]
        for block in range(3):
            head["w", block] = w_blocks[block]

    def pair(target, source):
        return target * (target + 1) // 2 + source

    def fb(target, source):
        return head["f", pair(target, source)]

    rows_of = lax.broadcasted_iota(jnp.int32, (NB, NB), 0)
    cols_of = lax.broadcasted_iota(jnp.int32, (NB, NB), 1)
    own_row = row * NQ + chip
    own_mask = jnp.logical_and(rows_of == own_row, cols_of // HALF == core)

    def own_share(block):
        lane = hl_ref[block : block + 1, :]
        return jnp.where(own_mask, jnp.concatenate([lane, lane], axis=1), 0.0)

    def adjoint(column, totals):
        inner = dot(fb(column, column).T, totals)
        inner = jnp.where(rows_of > cols_of, inner, jnp.where(rows_of == cols_of, 0.5 * inner, 0.0))
        mapped = dot(dot(head["w", column].T, inner), head["w", column])
        return 0.5 * (mapped + mapped.T)

    columns, terms, found, carried = {}, {}, {}, {}

    def trail(panel):
        wait(pr.at[panel], yx_recv.at[panel])
        total = y[panel, core, chip]
        for source in range(NQ - 1):
            total = total + pr[panel, source]
        gradient = b_ref[:, panel * NB : (panel + 1) * NB] - 2.0 * total
        for source in range(panel + 1, 3):
            gradient = gradient - 2.0 * dot(columns[source], fb(source, panel))
        columns[panel] = 0.5 * dot(gradient, head["w", panel])
        xt_ref[:, panel * NB : (panel + 1) * NB] = columns[panel]
        padded = jnp.concatenate([columns[panel], jnp.zeros((HALF - 24, NB), jnp.float32)], axis=0)
        turned = padded.T
        for source in range(panel + 1):
            own = f_ref[:, source * NB : (source + 1) * NB]
            own = jnp.concatenate([own, jnp.zeros((HALF - 24, NB), jnp.float32)], axis=0)
            terms[panel, source] = own_share(pair(panel, source)) - 2.0 * dot(turned, own)

    def put(panel, source, value):
        for half in range(2):
            nat[half, source] = value[:, half * HALF : (half + 1) * HALF]

    def stage(panel):
        if panel == 2:
            found[2, 2] = adjoint(2, terms[2, 2])
            carried[2, 1] = dot(terms[2, 1] - 2.0 * dot(found[2, 2], fb(2, 1)), head["w", 1])
            found[2, 1] = 0.5 * carried[2, 1]
            summed = dot(found[2, 1], fb(1, 0)) + dot(found[2, 2], fb(2, 0))
            carried[2, 0] = dot(terms[2, 0] - 2.0 * summed, head["w", 0])
            found[2, 0] = 0.5 * carried[2, 0]
        elif panel == 1:
            found[1, 1] = adjoint(1, terms[1, 1] - dot(carried[2, 1].T, fb(2, 1)))
            summed = dot(found[1, 1], fb(1, 0)) + dot(found[2, 1].T, fb(2, 0))
            carried[1, 0] = dot(terms[1, 0] - 2.0 * summed, head["w", 0])
            found[1, 0] = 0.5 * carried[1, 0]
        else:
            known = dot(carried[1, 0].T, fb(1, 0)) + dot(carried[2, 0].T, fb(2, 0))
            found[0, 0] = adjoint(0, terms[0, 0] - known)
        for source in range(panel + 1):
            for half in range(2):
                nat[half, pair(panel, source)] = found[panel, source][:, half * HALF : (half + 1) * HALF]
        first = pair(panel, 0)
        count = pl.ds(first, panel + 1)
        s_copies[panel] = remote(
            nat.at[other, count], nrecv.at[count], xs_sem.at[0, panel], xs_sem.at[1, panel], sibling
        )
        s_copies[panel].start()

    def scatter_col(panel):
        s_copies[panel].wait_recv()
        first = pair(panel, 0)
        for source in range(panel + 1):
            block = first + source
            for part in range(NQ):
                piece = nat[core, block, pl.ds(part, NZ, stride=NQ), :] + nrecv[block, pl.ds(part, NZ, stride=NQ), :]
                tsum[part, block] = piece
        count = pl.ds(first, panel + 1)

        def spread(step, carry):
            remote(
                tsum.at[lax.rem(chip + step, NQ), count], trecv.at[step - 1, count],
                xx_send.at[panel], xx_recv.at[panel], along_col(step),
            ).start()
            return carry

        lax.fori_loop(1, NQ, spread, 0)

    def scatter_row(panel):
        first = pair(panel, 0)
        count = pl.ds(first, panel + 1)
        wait(trecv.at[:, count], xx_recv.at[panel])
        total = tsum[chip, count]
        for source in range(NQ - 1):
            total = total + trecv[source, count]
        for source in range(panel + 1):
            zsend[:, first + source] = total[source].reshape(NZ, 1, HALF)

        def spread(step, carry):
            remote(
                zsend.at[lax.rem(row + step, NZ), count], zrecv.at[step - 1, count],
                xz_send.at[panel], xz_recv.at[panel], along_row(step),
            ).start()
            return carry

        lax.fori_loop(1, NZ, spread, 0)

    def finish(panel):
        first = pair(panel, 0)
        count = pl.ds(first, panel + 1)
        wait(zrecv.at[:, count], xz_recv.at[panel])
        for source in range(panel + 1):
            total = zsend[row, first + source]
            for step in range(NZ - 1):
                total = total + zrecv[step, first + source]
            head_ref[first + source : first + source + 1, :] = total

    if STOP >= 5:
        trail(2)
        stage(2)
        trail(1)
        stage(1)
        trail(0)
        stage(0)
    if STOP >= 6:
        scatter_col(2)
        scatter_col(1)
        scatter_col(0)
    if STOP >= 7:
        scatter_row(2)
        scatter_row(1)
        scatter_row(0)
        finish(2)
        finish(1)
        finish(0)

    wait(fz.at[:, pl.ds(0, NZ - 1)], ring_send)
    wait(zslot_f.at[pl.ds(0, NZ - 1)], hz_send)
    wait(zslot_i.at[pl.ds(0, NZ - 1)], hz_send)
    wait(hx.at[0, pl.ds(0, NQ - 1)], hx_send)
    head_copy.wait_send()
    for panel in range(3):
        first = pair(panel, 0)
        count = pl.ds(first, panel + 1)
        if STOP >= 2:
            y_copies[panel].wait_send()
            if STOP < 3:
                y_copies[panel].wait_recv()
        if STOP >= 3:
            wait(pr.at[panel], yx_send.at[panel])
            if STOP < 5:
                wait(pr.at[panel], yx_recv.at[panel])
        if STOP >= 5:
            s_copies[panel].wait_send()
            if STOP < 6:
                s_copies[panel].wait_recv()
        if STOP >= 6:
            wait(trecv.at[:, count], xx_send.at[panel])
            if STOP < 7:
                wait(trecv.at[:, count], xx_recv.at[panel])
        if STOP >= 7:
            wait(zrecv.at[:, count], xz_send.at[panel])
    if 1 < STOP < 5:
        xt_ref[...] = y[0, 0, 0, :, :1] + jnp.zeros_like(xt_ref)
    if 1 < STOP < 7:
        head_ref[...] = nat[0, 0, :6, :]


def scratch():
    f32 = jnp.float32
    dma = pltpu.SemaphoreType.DMA
    return [
        pltpu.VMEM((2, NQ * 24, NZ * 24), f32),
        pltpu.VMEM((3, NZ, 24, NB), f32),
        pltpu.VMEM((3, 2, NQ, 24, NB), f32),
        pltpu.VMEM((3, NQ, 24, NB), f32),
        pltpu.VMEM((3, NQ - 1, 24, NB), f32),
        pltpu.VMEM((NZ, 6, HALF), f32),
        pltpu.VMEM((NZ, 3, HALF), f32),
        pltpu.VMEM((2, NQ, 9, NZ, HALF), f32),
        pltpu.VMEM((768, NZ * 24), f32),
        pltpu.VMEM((2, 9, NB, HALF), f32),
        pltpu.VMEM((6, NB, HALF), f32),
        pltpu.VMEM((NQ, 6, NZ, HALF), f32),
        pltpu.VMEM((NQ - 1, 6, NZ, HALF), f32),
        pltpu.VMEM((NZ, 6, 1, HALF), f32),
        pltpu.VMEM((NZ - 1, 6, 1, HALF), f32),
        dma,
        dma((2, 3, RING)),
        dma,
        dma((2,)),
        dma,
        dma,
        dma((2,)),
        dma((2, 3)),
        dma((3,)),
        dma((3,)),
        dma((2, 3)),
        dma((3,)),
        dma((3,)),
        dma((3,)),
        dma((3,)),
    ]


def body(trail_adj, trail_factor, trail_lbar, head_factor, head_inverse, head_lbar):
    return tuple(
        pl.pallas_call(
            kernel,
            out_shape=(
                jax.ShapeDtypeStruct(trail_lbar.shape, jnp.float32),
                jax.ShapeDtypeStruct(head_lbar.shape, jnp.float32),
            ),
            in_specs=[pl.BlockSpec(memory_space=pltpu.VMEM)] * 6,
            out_specs=(pl.BlockSpec(memory_space=pltpu.VMEM), pl.BlockSpec(memory_space=pltpu.VMEM)),
            scratch_shapes=scratch(),
            compiler_params=pltpu.CompilerParams(
                collective_id=0, has_side_effects=True, vmem_limit_bytes=48 * 1024 * 1024
            ),
            name="chol_adjoint",
        )(trail_adj, trail_factor, trail_lbar, head_factor, head_inverse, head_lbar)
    )


def solution(mesh):
    in_specs = (
        P(None, "col", "row"),
        P(("row", "col"), None),
        P(("row", "col"), None),
        P(None, ("row", "col")),
        P(None, ("row", "col")),
        P(None, ("row", "col")),
    )
    out_specs = (P(("row", "col"), None), P(None, ("row", "col")))
    return jax.shard_map(body, mesh=mesh, in_specs=in_specs, out_specs=out_specs, check_vma=False)
```

```python
import functools

import jax
import jax.numpy as jnp
from jax import lax
from jax.experimental import pallas as pl
from jax.experimental.pallas import tpu as pltpu
from jax.sharding import PartitionSpec as P

MESH = pl.DeviceIdType.MESH
NB = 256
HALF = 128
NZ = 16
NQ = 16
REACH = 8
PLANE = (
    (1, 0), (0, 1), (3, 0), (0, 3), (1, 1), (3, 3), (1, 3), (3, 1),
    (2, 0), (0, 2), (2, 1), (1, 2), (2, 3), (3, 2), (2, 2),
)


def dot(left, right):
    return jnp.dot(left, right, precision=lax.Precision.HIGH, preferred_element_type=jnp.float32)


def kernel(
    z_hbm, f_hbm, b_hbm, hf_hbm, hi_hbm, hl_hbm, xt_ref, head_ref,
    z_ref, b_ref, hf_ref, hi_ref, hl_ref, hf_side, pack,
    zt, fz, fcol, q, qr, y, yr, pr, zslot, hx, hm, nat, nrecv, tsum, trecv, zsend, zrecv,
    in_sem, side_sem, ring_send, ring_recv, fc_send, fc_recv, fs_sem, q_send, q_recv, hz_send, hz_recv, hx_send, hx_recv, hs_sem, ys_sem, yx_send, yx_recv,
    xs_sem, xx_send, xx_recv, xz_send, xz_recv,
):
    row = lax.axis_index("row")
    col = lax.axis_index("col")
    core = lax.rem(col, 2)
    chip = col // 2
    other = 1 - core
    sibling = (row, chip * 2 + other)

    def along_row(step):
        return (lax.rem(row + step, NZ), col)

    chip_x, chip_y = chip // 4, lax.rem(chip, 4)

    def plane(index):
        first, second = PLANE[index]
        move_x = first * (1 - core) + second * core
        move_y = second * (1 - core) + first * core
        return lax.rem(chip_x + move_x, 4) * 4 + lax.rem(chip_y + move_y, 4)

    def along_col(index):
        return (row, plane(index) * 2 + core)

    def remote(src, dst, send, recv, target):
        return pltpu.make_async_remote_copy(
            src_ref=src, dst_ref=dst, send_sem=send, recv_sem=recv, device_id=target, device_id_type=MESH
        )

    def wait(region, sem):
        pltpu.make_async_copy(region, region, sem).wait()

    pending = {}

    def landed(key):
        pending.pop(key)()

    def later(key, region, sem):
        pending[key] = functools.partial(wait, region, sem)

    inputs = [
        pltpu.make_async_copy(hf_hbm, hf_ref, in_sem.at[0]),
        pltpu.make_async_copy(hi_hbm, hi_ref, in_sem.at[1]),
        pltpu.make_async_copy(f_hbm.at[:, pl.ds(0, NB)], fz.at[0, row], in_sem.at[2]),
        pltpu.make_async_copy(f_hbm.at[:, pl.ds(NB, NB)], fz.at[1, row], in_sem.at[3]),
        pltpu.make_async_copy(f_hbm.at[:, pl.ds(2 * NB, NB)], fz.at[2, row], in_sem.at[4]),
        pltpu.make_async_copy(z_hbm, z_ref, in_sem.at[5]),
        pltpu.make_async_copy(b_hbm, b_ref, in_sem.at[6]),
        pltpu.make_async_copy(hl_hbm, hl_ref, in_sem.at[7]),
    ]
    for copy in inputs:
        copy.start()

    barrier = pltpu.get_barrier_semaphore()
    pl.semaphore_signal(barrier, inc=1, device_id=sibling, device_id_type=MESH)
    for index in range(NQ - 1):
        pl.semaphore_signal(barrier, inc=1, device_id=along_col(index), device_id_type=MESH)

    def greet(step, carry):
        pl.semaphore_signal(barrier, inc=1, device_id=along_row(step), device_id_type=MESH)
        return carry

    lax.fori_loop(1, NZ, greet, 0)
    for copy in inputs[:5]:
        copy.wait()
    pack[0:1] = hf_ref[1:2]
    pack[1:3] = hf_ref[3:5]
    pack[3:6] = hi_ref[...]
    zslot[row] = pack[...]
    pl.semaphore_wait(barrier, 31)

    def ring_block(panel, way, distance, slot):
        if distance == REACH:
            return fz.at[panel, slot, :, pl.ds(way * HALF, HALF)]
        return fz.at[panel, slot]

    def ring_landed(panel, way, distance):
        landed(("ring", way, panel, distance))

    def ring_step(step):
        for panel in (1, 0):
            for way in (0, 1):
                if step > 0:
                    ring_landed(panel, way, 2 * step)
                for ahead in (2, 1):
                    distance = 2 * step + ahead
                    if way == 0:
                        slot, target = lax.rem(row - 2 * step + NZ, NZ), along_row(ahead)
                    else:
                        slot, target = lax.rem(row + 2 * step, NZ), along_row(NZ - ahead)
                    block = ring_block(panel, way, distance, slot)
                    remote(block, block, ring_send, ring_recv.at[way, panel, distance - 1], target).start()
                    later(
                        ("ring", way, panel, distance), ring_block(panel, way, distance, 0),
                        ring_recv.at[way, panel, distance - 1],
                    )

    def head_send(step, carry):
        remote(pack, zslot.at[row], hz_send, hz_recv, along_row(step)).start()
        return carry

    def turn(slab):
        rows = z_ref[:, :, slab * HALF : (slab + 1) * HALF].reshape(NZ * 24, HALF)
        hm[slab * HALF : (slab + 1) * HALF, :] = rows.T

    head = {}
    y_copies, s_copies, h_copies = {}, {}, {}

    def head_row():
        lax.fori_loop(1, NZ, head_send, 0)
        copy = remote(hf_ref, hf_side, side_sem.at[0], side_sem.at[1], sibling)
        copy.start()
        pending["side"], pending["side_out"] = copy.wait_recv, copy.wait_send
        later("hz", zslot.at[pl.ds(0, NZ - 1)], hz_recv)
        later("hz_out", zslot.at[pl.ds(0, NZ - 1)], hz_send)

    def turn_all():
        for copy in inputs[5:]:
            copy.wait()
        for slab in range(6):
            turn(slab)

    def head_col():
        landed("hz")
        for block in range(6):
            hx[core, chip, block] = zslot[:, block, :]
        for index in range(NQ - 1):
            remote(hx.at[core, chip], hx.at[core, chip], hx_send, hx_recv, along_col(index)).start()
        later("hx", hx.at[0, pl.ds(0, NQ - 1)], hx_recv)
        later("hx_out", hx.at[0, pl.ds(0, NQ - 1)], hx_send)

    def column_gather():
        fcol[core, chip] = fz[2, row]
        own = fcol.at[core, chip]
        for index in range(NQ - 1):
            remote(fz.at[2, row], own, fc_send, fc_recv, along_col(index)).start()
        later("fc", fcol.at[0, pl.ds(0, NQ - 1)], fc_recv)
        later("fc_out", fcol.at[0, pl.ds(0, NQ - 1)], fc_send)

    def column_sibling():
        landed("fc")
        copy = remote(fcol.at[core], fcol.at[core], fs_sem.at[0], fs_sem.at[1], sibling)
        copy.start()
        pending["fs"], pending["fs_out"] = copy.wait_recv, copy.wait_send

    def reduce_send(way, distance):
        slot = lax.rem(row + (NZ - distance if way else distance), NZ)
        ahead = 1 if distance % 2 else 2
        target = along_row(NZ - ahead if way else ahead)
        if distance == REACH:
            source = q.at[slot, :, pl.ds(way * HALF, HALF)]
            there = qr.at[way, distance - 1, :, pl.ds(way * HALF, HALF)]
        else:
            source, there = q.at[slot], qr.at[way, distance - 1]
        remote(source, there, q_send, q_recv.at[way, distance - 1], target).start()
        later(("q", way, distance), there, q_recv.at[way, distance - 1])

    def multiply_rows():
        landed("fs")
        factor = jnp.concatenate([fcol[side, part] for part in range(NQ) for side in range(2)], axis=0)
        q[...] = dot(z_ref[...].reshape(NZ * 24, NZ * 48), factor).reshape(NZ, 24, NB)
        for distance in (8, 7, 5, 3, 1):
            for way in range(2):
                reduce_send(way, distance)
        later("q_out", q.at[pl.ds(0, NZ - 1)], q_send)

    def reduce_step(distance):
        for way in range(2):
            slot = lax.rem(row + (NZ - distance if way else distance), NZ)
            landed(("q", way, distance + 1))
            landed(("q", way, distance + 2))
            if distance + 2 == REACH:
                lanes_of = slice(way * HALF, (way + 1) * HALF)
                q[slot] = q[slot] + qr[way, distance]
                q[slot, :, lanes_of] = q[slot, :, lanes_of] + qr[way, distance + 1, :, lanes_of]
            else:
                q[slot] = q[slot] + qr[way, distance] + qr[way, distance + 1]
            reduce_send(way, distance)

    def arrange():
        for half in range(2):
            for part in range(NQ):
                start = (part * 2 + half) * 24
                zt[half, part * 24 : (part + 1) * 24, :] = hm[start : start + 24, :]

    def multiply(panel):
        for key in [key for key in pending if key[0] == "ring" and key[2] == panel]:
            landed(key)
        factor = fz[panel].reshape(NZ * 24, NB)
        for side in (other, core):
            product = dot(zt[side], factor)
            y[panel, side] = product.reshape(NQ, 24, NB)
            if side is other:
                copy = remote(y.at[panel, side], yr.at[panel], ys_sem.at[0, panel], ys_sem.at[1, panel], sibling)
                copy.start()
                pending["ys", panel], pending["ys_out", panel] = copy.wait_recv, copy.wait_send

    def scatter_product(panel):
        landed(("ys", panel))
        y[panel, core] = y[panel, core] + yr[panel]
        for index in range(NQ - 1):
            remote(
                y.at[panel, core, plane(index)], pr.at[panel, index], yx_send.at[panel], yx_recv.at[panel],
                along_col(index),
            ).start()
        later(("yx", panel), pr.at[panel], yx_recv.at[panel])
        later(("yx_out", panel), pr.at[panel], yx_send.at[panel])

    def product_total(panel):
        if panel == 2:
            total = q[row]
            for way in range(2):
                landed(("q", way, 1))
                landed(("q", way, 2))
                total = total + qr[way, 0] + qr[way, 1]
            return total
        landed(("yx", panel))
        total = y[panel, core, chip]
        for source in range(NQ - 1):
            total = total + pr[panel, source]
        return total

    def head_sibling():
        landed("hx")
        copy = remote(hx.at[core], hx.at[core], hs_sem.at[0], hs_sem.at[1], sibling)
        copy.start()
        pending["hs"], pending["hs_out"] = copy.wait_recv, copy.wait_send

    def head_arrange():
        landed("hs")
        for block in range(6):
            halves = []
            for half in range(2):
                nat[half, block] = hx[half, :, block].reshape(NB, HALF)
                pieces = [nat[half, block, pl.ds(z, NQ, stride=NQ), :] for z in range(NZ)]
                halves.append(jnp.concatenate(pieces, axis=0))
            head[("f10", "f20", "f21", "w0", "w1", "w2")[block]] = jnp.concatenate(halves, axis=1)

    def pair(target, source):
        return target * (target + 1) // 2 + source

    columns, gradients, terms, bracket, found = {}, {}, {}, {}, {}
    rows_of = lax.broadcasted_iota(jnp.int32, (NB, NB), 0)
    cols_of = lax.broadcasted_iota(jnp.int32, (NB, NB), 1)
    top = lax.broadcasted_iota(jnp.int32, (8, NB), 0) == 0
    lanes = lax.broadcasted_iota(jnp.int32, (8, NB), 1)
    own_lanes = jnp.logical_and(top, lanes // HALF == core)
    other_lanes = jnp.logical_and(top, lanes // HALF == other)

    def wide(ref, block):
        half = ref[block : block + 1, :]
        return jnp.broadcast_to(jnp.concatenate([half, half], axis=1), (8, NB))

    def tall(rows, extra):
        return jnp.concatenate([rows, extra, jnp.zeros((HALF - 32, NB), jnp.float32)], axis=0)

    def lbar_row(block):
        return jnp.where(own_lanes, wide(hl_ref, block), 0.0)

    def factor_row(block):
        return jnp.where(own_lanes, wide(hf_ref, block), jnp.where(other_lanes, wide(hf_side, block), 0.0))

    def start_gradient(panel):
        gradient = b_ref[:, panel * NB : (panel + 1) * NB]
        for source in range(panel + 1, 3):
            gradient = gradient - 2.0 * dot(columns[source], head["f" + str(source) + str(panel)])
        gradients[panel] = gradient

    def trail(panel):
        if panel == 2:
            landed("side")
        gradient = gradients[panel] - 2.0 * product_total(panel)
        diagonal = pair(panel, panel)
        left = tall(gradient, factor_row(diagonal)).T
        terms[panel, panel] = dot(left, tall(-fz[panel, row], lbar_row(diagonal)))
        columns[panel] = 0.5 * dot(gradient, head["w" + str(panel)])
        xt_ref[:, panel * NB : (panel + 1) * NB] = columns[panel]
        if panel > 0:
            unit = jnp.where(jnp.logical_and(top, lanes == row * NQ + chip), 1.0, 0.0)
            left = tall(columns[panel], unit).T
            for source in range(panel):
                terms[panel, source] = dot(left, tall(-2.0 * fz[source, row], lbar_row(pair(panel, source))))

    def diagonal_block(column, inner):
        lower = jnp.where(rows_of > cols_of, inner, jnp.where(rows_of == cols_of, 0.5 * inner, 0.0))
        inverse = head["w" + str(column)]
        return dot(inverse.T, dot(0.5 * (lower + lower.T), inverse))

    def stage(panel):
        if panel == 2:
            found[2, 2] = diagonal_block(2, terms[2, 2])
            bracket[2, 1] = terms[2, 1] - 2.0 * dot(found[2, 2], head["f21"])
            found[2, 1] = 0.5 * dot(bracket[2, 1], head["w1"])
            bracket[2, 0] = terms[2, 0] - 2.0 * (dot(found[2, 1], head["f10"]) + dot(found[2, 2], head["f20"]))
            found[2, 0] = 0.5 * dot(bracket[2, 0], head["w0"])
        elif panel == 1:
            found[1, 1] = diagonal_block(1, terms[1, 1] - dot(bracket[2, 1].T, head["f21"]))
            bracket[1, 0] = terms[1, 0] - 2.0 * (dot(found[1, 1], head["f10"]) + dot(found[2, 1].T, head["f20"]))
            found[1, 0] = 0.5 * dot(bracket[1, 0], head["w0"])
            terms["known"] = dot(bracket[1, 0].T, head["f10"]) + dot(bracket[2, 0].T, head["f20"])
        else:
            found[0, 0] = diagonal_block(0, terms[0, 0] - terms["known"])
        for source in range(panel + 1):
            for half in range(2):
                nat[half, pair(panel, source)] = found[panel, source][:, half * HALF : (half + 1) * HALF]
        count = pl.ds(pair(panel, 0), panel + 1)
        copy = remote(nat.at[other, count], nrecv.at[count], xs_sem.at[0, panel], xs_sem.at[1, panel], sibling)
        copy.start()
        pending["xs", panel], pending["xs_out", panel] = copy.wait_recv, copy.wait_send

    def scatter_result(panel):
        landed(("xs", panel))
        first = pair(panel, 0)
        for source in range(panel + 1):
            block = first + source
            for part in range(NQ):
                rows = pl.ds(part, NZ, stride=NQ)
                tsum[part, block] = nat[core, block, rows, :] + nrecv[block, rows, :]
        count = pl.ds(first, panel + 1)
        for index in range(NQ - 1):
            remote(
                tsum.at[plane(index), count], trecv.at[index, count], xx_send.at[panel], xx_recv.at[panel],
                along_col(index),
            ).start()
        later(("xx", panel), trecv.at[:, count], xx_recv.at[panel])
        later(("xx_out", panel), trecv.at[:, count], xx_send.at[panel])

    def result_row(panel):
        landed(("xx", panel))
        first = pair(panel, 0)
        count = pl.ds(first, panel + 1)
        total = tsum[chip, count]
        for source in range(NQ - 1):
            total = total + trecv[source, count]
        for source in range(panel + 1):
            zsend[:, first + source] = total[source].reshape(NZ, 1, HALF)

        def spread(step, carry):
            remote(
                zsend.at[lax.rem(row + step, NZ), count], zrecv.at[step - 1, count],
                xz_send.at[panel], xz_recv.at[panel], along_row(step),
            ).start()
            return carry

        lax.fori_loop(1, NZ, spread, 0)
        later(("xz", panel), zrecv.at[:, count], xz_recv.at[panel])
        later(("xz_out", panel), zrecv.at[:, count], xz_send.at[panel])

    def finish(panel):
        first = pair(panel, 0)
        count = pl.ds(first, panel + 1)
        landed(("xz", panel))
        for source in range(panel + 1):
            total = zsend[row, first + source]
            for step in range(NZ - 1):
                total = total + zrecv[step, first + source]
            head_ref[first + source : first + source + 1, :] = total

    phases = [
        (column_gather,), (head_row,), (ring_step, 0), (turn_all,), (ring_step, 1), (column_sibling,), (head_col,),
        (ring_step, 2), (arrange,), (multiply_rows,), (ring_step, 3), (reduce_step, 6),
        (multiply, 1), (reduce_step, 4), (multiply, 0), (scatter_product, 1), (scatter_product, 0), (head_sibling,),
        (reduce_step, 2), (head_arrange,), (start_gradient, 2),
        (trail, 2), (stage, 2), (start_gradient, 1), (scatter_result, 2), (trail, 1), (start_gradient, 0), (stage, 1),
        (trail, 0), (stage, 0), (scatter_result, 1), (scatter_result, 0),
        (result_row, 2), (result_row, 1), (result_row, 0), (finish, 2), (finish, 1), (finish, 0),
    ]
    for phase, *argument in phases:
        phase(*argument)
    later("ring_out", fz.at[pl.ds(0, 2), pl.ds(0, NZ - 1)], ring_send)

    for key in list(pending):
        landed(key)


def scratch():
    f32 = jnp.float32
    dma = pltpu.SemaphoreType.DMA
    return [
        pltpu.VMEM((NZ, 24, 768), f32),
        pltpu.VMEM((24, 768), f32),
        pltpu.VMEM((6, HALF), f32),
        pltpu.VMEM((3, HALF), f32),
        pltpu.VMEM((6, HALF), f32),
        pltpu.VMEM((6, HALF), f32),
        pltpu.VMEM((6, HALF), f32),
        pltpu.VMEM((2, NQ * 24, NZ * 24), f32),
        pltpu.VMEM((3, NZ, 24, NB), f32),
        pltpu.VMEM((2, NQ, 24, NB), f32),
        pltpu.VMEM((NZ, 24, NB), f32),
        pltpu.VMEM((2, REACH, 24, NB), f32),
        pltpu.VMEM((2, 2, NQ, 24, NB), f32),
        pltpu.VMEM((2, NQ, 24, NB), f32),
        pltpu.VMEM((2, NQ - 1, 24, NB), f32),
        pltpu.VMEM((NZ, 6, HALF), f32),
        pltpu.VMEM((2, NQ, 6, NZ, HALF), f32),
        pltpu.VMEM((768, NZ * 24), f32),
        pltpu.VMEM((2, 6, NB, HALF), f32),
        pltpu.VMEM((6, NB, HALF), f32),
        pltpu.VMEM((NQ, 6, NZ, HALF), f32),
        pltpu.VMEM((NQ - 1, 6, NZ, HALF), f32),
        pltpu.VMEM((NZ, 6, 1, HALF), f32),
        pltpu.VMEM((NZ - 1, 6, 1, HALF), f32),
        dma((8,)),
        dma((2,)),
        dma,
        dma((2, 2, REACH)),
        dma,
        dma,
        dma((2,)),
        dma,
        dma((2, REACH)),
        dma,
        dma,
        dma,
        dma,
        dma((2,)),
        dma((2, 2)),
        dma((2,)),
        dma((2,)),
        dma((2, 3)),
        dma((3,)),
        dma((3,)),
        dma((3,)),
        dma((3,)),
    ]


def body(trail_adj, trail_factor, trail_lbar, head_factor, head_inverse, head_lbar):
    return tuple(
        pl.pallas_call(
            kernel,
            out_shape=(
                pltpu.VMEM(trail_lbar.shape, jnp.float32),
                pltpu.VMEM(head_lbar.shape, jnp.float32),
            ),
            in_specs=[pl.BlockSpec(memory_space=pltpu.HBM)] * 6,
            out_specs=(pl.BlockSpec(memory_space=pltpu.VMEM), pl.BlockSpec(memory_space=pltpu.VMEM)),
            scratch_shapes=scratch(),
            compiler_params=pltpu.CompilerParams(
                collective_id=0, has_side_effects=True, vmem_limit_bytes=60 * 1024 * 1024
            ),
            name="chol_adjoint",
        )(trail_adj, trail_factor, trail_lbar, head_factor, head_inverse, head_lbar)
    )


def solution(mesh):
    in_specs = (
        P(None, "col", "row"),
        P(("row", "col"), None),
        P(("row", "col"), None),
        P(None, ("row", "col")),
        P(None, ("row", "col")),
        P(None, ("row", "col")),
    )
    out_specs = (P(("row", "col"), None), P(None, ("row", "col")))
    return jax.shard_map(body, mesh=mesh, in_specs=in_specs, out_specs=out_specs, check_vma=False)
```

```python
import functools

import jax
import jax.numpy as jnp
from jax import lax
from jax.experimental import pallas as pl
from jax.experimental.pallas import tpu as pltpu
from jax.sharding import PartitionSpec as P

MESH = pl.DeviceIdType.MESH
NB = 256
HALF = 128
NZ = 16
NQ = 16
REACH = 8
PLANE = (
    (1, 0), (0, 1), (3, 0), (0, 3), (1, 1), (3, 3), (1, 3), (3, 1),
    (2, 0), (0, 2), (2, 1), (1, 2), (2, 3), (3, 2), (2, 2),
)


def dot(left, right):
    return jnp.dot(left, right, precision=lax.Precision.HIGH, preferred_element_type=jnp.float32)


def kernel(
    z_hbm, f_hbm, b_hbm, hf_hbm, hi_hbm, hl_hbm, xt_ref, head_ref,
    z_ref, b_ref, hf_ref, hi_ref, hl_ref, hf_side, pack,
    zt, fz, fcol, q, qr, y, yr, pr, zslot, hx, hm, nat, nrecv, tsum, trecv, zsend, zrecv,
    in_sem, side_sem, ring_send, ring_recv, fc_send, fc_recv, fs_sem, q_send, q_recv, hz_send, hz_recv, hx_send, hx_recv, hs_sem, ys_sem, yx_send, yx_recv,
    xs_sem, xx_send, xx_recv, xz_send, xz_recv,
):
    row = lax.axis_index("row")
    col = lax.axis_index("col")
    core = lax.rem(col, 2)
    chip = col // 2
    other = 1 - core
    sibling = (row, chip * 2 + other)

    def along_row(step):
        return (lax.rem(row + step, NZ), col)

    chip_x, chip_y = chip // 4, lax.rem(chip, 4)

    def plane(index):
        first, second = PLANE[index]
        move_x = first * (1 - core) + second * core
        move_y = second * (1 - core) + first * core
        return lax.rem(chip_x + move_x, 4) * 4 + lax.rem(chip_y + move_y, 4)

    def along_col(index):
        return (row, plane(index) * 2 + core)

    def remote(src, dst, send, recv, target):
        return pltpu.make_async_remote_copy(
            src_ref=src, dst_ref=dst, send_sem=send, recv_sem=recv, device_id=target, device_id_type=MESH
        )

    def wait(region, sem):
        pltpu.make_async_copy(region, region, sem).wait()

    pending = {}

    def landed(key):
        pending.pop(key)()

    def later(key, region, sem):
        pending[key] = functools.partial(wait, region, sem)

    inputs = [
        pltpu.make_async_copy(hf_hbm, hf_ref, in_sem.at[0]),
        pltpu.make_async_copy(hi_hbm, hi_ref, in_sem.at[1]),
        pltpu.make_async_copy(f_hbm.at[:, pl.ds(0, NB)], fz.at[0, row], in_sem.at[2]),
        pltpu.make_async_copy(f_hbm.at[:, pl.ds(NB, NB)], fz.at[1, row], in_sem.at[3]),
        pltpu.make_async_copy(f_hbm.at[:, pl.ds(2 * NB, NB)], fz.at[2, row], in_sem.at[4]),
        pltpu.make_async_copy(z_hbm, z_ref, in_sem.at[5]),
        pltpu.make_async_copy(b_hbm, b_ref, in_sem.at[6]),
        pltpu.make_async_copy(hl_hbm, hl_ref, in_sem.at[7]),
    ]
    for copy in inputs:
        copy.start()

    barrier = pltpu.get_barrier_semaphore()
    pl.semaphore_signal(barrier, inc=1, device_id=sibling, device_id_type=MESH)
    for index in range(NQ - 1):
        pl.semaphore_signal(barrier, inc=1, device_id=along_col(index), device_id_type=MESH)

    def greet(step, carry):
        pl.semaphore_signal(barrier, inc=1, device_id=along_row(step), device_id_type=MESH)
        return carry

    lax.fori_loop(1, NZ, greet, 0)
    for copy in inputs[:5]:
        copy.wait()
    pack[0:1] = hf_ref[1:2]
    pack[1:3] = hf_ref[3:5]
    pack[3:6] = hi_ref[...]
    zslot[row] = pack[...]
    pl.semaphore_wait(barrier, 31)

    def ring_block(panel, way, distance, slot):
        if distance == REACH:
            return fz.at[panel, slot, :, pl.ds(way * HALF, HALF)]
        return fz.at[panel, slot]

    def ring_landed(panel, way, distance):
        landed(("ring", way, panel, distance))

    def ring_step(step):
        for panel in (1, 0):
            for way in (0, 1):
                if step > 0:
                    ring_landed(panel, way, 2 * step)
                for ahead in (2, 1):
                    distance = 2 * step + ahead
                    if way == 0:
                        slot, target = lax.rem(row - 2 * step + NZ, NZ), along_row(ahead)
                    else:
                        slot, target = lax.rem(row + 2 * step, NZ), along_row(NZ - ahead)
                    block = ring_block(panel, way, distance, slot)
                    remote(block, block, ring_send, ring_recv.at[way, panel, distance - 1], target).start()
                    later(
                        ("ring", way, panel, distance), ring_block(panel, way, distance, 0),
                        ring_recv.at[way, panel, distance - 1],
                    )

    def head_send(step, carry):
        remote(pack, zslot.at[row], hz_send, hz_recv, along_row(step)).start()
        return carry

    def turn(slab):
        rows = z_ref[:, :, slab * HALF : (slab + 1) * HALF].reshape(NZ * 24, HALF)
        hm[slab * HALF : (slab + 1) * HALF, :] = rows.T

    head = {}
    y_copies, s_copies, h_copies = {}, {}, {}

    def head_row():
        lax.fori_loop(1, NZ, head_send, 0)
        copy = remote(hf_ref, hf_side, side_sem.at[0], side_sem.at[1], sibling)
        copy.start()
        pending["side"], pending["side_out"] = copy.wait_recv, copy.wait_send
        later("hz", zslot.at[pl.ds(0, NZ - 1)], hz_recv)
        later("hz_out", zslot.at[pl.ds(0, NZ - 1)], hz_send)

    def turn_all():
        for copy in inputs[5:]:
            copy.wait()
        for slab in range(6):
            turn(slab)

    def head_col():
        landed("hz")
        for block in range(6):
            hx[core, chip, block] = zslot[:, block, :]
        for index in range(NQ - 1):
            remote(hx.at[core, chip], hx.at[core, chip], hx_send, hx_recv, along_col(index)).start()
        later("hx", hx.at[0, pl.ds(0, NQ - 1)], hx_recv)
        later("hx_out", hx.at[0, pl.ds(0, NQ - 1)], hx_send)

    def column_gather():
        fcol[core, chip] = fz[2, row]
        own = fcol.at[core, chip]
        for index in range(NQ - 1):
            remote(fz.at[2, row], own, fc_send, fc_recv, along_col(index)).start()
        later("fc", fcol.at[0, pl.ds(0, NQ - 1)], fc_recv)
        later("fc_out", fcol.at[0, pl.ds(0, NQ - 1)], fc_send)

    def column_sibling():
        landed("fc")
        copy = remote(fcol.at[core], fcol.at[core], fs_sem.at[0], fs_sem.at[1], sibling)
        copy.start()
        pending["fs"], pending["fs_out"] = copy.wait_recv, copy.wait_send

    def reduce_send(way, distance):
        slot = lax.rem(row + (NZ - distance if way else distance), NZ)
        ahead = 1 if distance % 2 else 2
        target = along_row(NZ - ahead if way else ahead)
        if distance == REACH:
            source = q.at[slot, :, pl.ds(way * HALF, HALF)]
            there = qr.at[way, distance - 1, :, pl.ds(way * HALF, HALF)]
        else:
            source, there = q.at[slot], qr.at[way, distance - 1]
        remote(source, there, q_send, q_recv.at[way, distance - 1], target).start()
        later(("q", way, distance), there, q_recv.at[way, distance - 1])

    def multiply_rows():
        landed("fs")
        factor = jnp.concatenate([fcol[side, part] for part in range(NQ) for side in range(2)], axis=0)
        q[...] = dot(z_ref[...].reshape(NZ * 24, NZ * 48), factor).reshape(NZ, 24, NB)
        for distance in (8, 7, 5, 3, 1):
            for way in range(2):
                reduce_send(way, distance)
        later("q_out", q.at[pl.ds(0, NZ - 1)], q_send)

    def reduce_step(distance):
        for way in range(2):
            slot = lax.rem(row + (NZ - distance if way else distance), NZ)
            landed(("q", way, distance + 1))
            landed(("q", way, distance + 2))
            if distance + 2 == REACH:
                lanes_of = slice(way * HALF, (way + 1) * HALF)
                q[slot] = q[slot] + qr[way, distance]
                q[slot, :, lanes_of] = q[slot, :, lanes_of] + qr[way, distance + 1, :, lanes_of]
            else:
                q[slot] = q[slot] + qr[way, distance] + qr[way, distance + 1]
            reduce_send(way, distance)

    def arrange():
        for half in range(2):
            for part in range(NQ):
                start = (part * 2 + half) * 24
                zt[half, part * 24 : (part + 1) * 24, :] = hm[start : start + 24, :]

    def multiply(panel):
        for key in [key for key in pending if key[0] == "ring" and key[2] == panel]:
            landed(key)
        factor = fz[panel].reshape(NZ * 24, NB)
        for side in (other, core):
            product = dot(zt[side], factor)
            y[panel, side] = product.reshape(NQ, 24, NB)
            if side is other:
                copy = remote(y.at[panel, side], yr.at[panel], ys_sem.at[0, panel], ys_sem.at[1, panel], sibling)
                copy.start()
                pending["ys", panel], pending["ys_out", panel] = copy.wait_recv, copy.wait_send

    def scatter_product(panel):
        landed(("ys", panel))
        y[panel, core] = y[panel, core] + yr[panel]
        for index in range(NQ - 1):
            remote(
                y.at[panel, core, plane(index)], pr.at[panel, index], yx_send.at[panel], yx_recv.at[panel],
                along_col(index),
            ).start()
        later(("yx", panel), pr.at[panel], yx_recv.at[panel])
        later(("yx_out", panel), pr.at[panel], yx_send.at[panel])

    def product_total(panel):
        if panel == 2:
            total = q[row]
            for way in range(2):
                landed(("q", way, 1))
                landed(("q", way, 2))
                total = total + qr[way, 0] + qr[way, 1]
            return total
        landed(("yx", panel))
        total = y[panel, core, chip]
        for source in range(NQ - 1):
            total = total + pr[panel, source]
        return total

    def head_sibling():
        landed("hx")
        copy = remote(hx.at[core], hx.at[core], hs_sem.at[0], hs_sem.at[1], sibling)
        copy.start()
        pending["hs"], pending["hs_out"] = copy.wait_recv, copy.wait_send

    def head_arrange():
        landed("hs")
        for block in range(6):
            halves = []
            for half in range(2):
                nat[half, block] = hx[half, :, block].reshape(NB, HALF)
                pieces = [nat[half, block, pl.ds(z, NQ, stride=NQ), :] for z in range(NZ)]
                halves.append(jnp.concatenate(pieces, axis=0))
            head[("f10", "f20", "f21", "w0", "w1", "w2")[block]] = jnp.concatenate(halves, axis=1)

    def pair(target, source):
        return target * (target + 1) // 2 + source

    columns, gradients, terms, bracket, found = {}, {}, {}, {}, {}
    rows_of = lax.broadcasted_iota(jnp.int32, (NB, NB), 0)
    cols_of = lax.broadcasted_iota(jnp.int32, (NB, NB), 1)
    top = lax.broadcasted_iota(jnp.int32, (8, NB), 0) == 0
    lanes = lax.broadcasted_iota(jnp.int32, (8, NB), 1)
    own_lanes = jnp.logical_and(top, lanes // HALF == core)
    other_lanes = jnp.logical_and(top, lanes // HALF == other)

    def wide(ref, block):
        half = ref[block : block + 1, :]
        return jnp.broadcast_to(jnp.concatenate([half, half], axis=1), (8, NB))

    def tall(rows, extra):
        return jnp.concatenate([rows, extra, jnp.zeros((HALF - 32, NB), jnp.float32)], axis=0)

    def lbar_row(block):
        return jnp.where(own_lanes, wide(hl_ref, block), 0.0)

    def factor_row(block):
        return jnp.where(own_lanes, wide(hf_ref, block), jnp.where(other_lanes, wide(hf_side, block), 0.0))

    def start_gradient(panel):
        gradient = b_ref[:, panel * NB : (panel + 1) * NB]
        for source in range(panel + 1, 3):
            gradient = gradient - 2.0 * dot(columns[source], head["f" + str(source) + str(panel)])
        gradients[panel] = gradient

    def trail(panel):
        if panel == 2:
            landed("side")
        gradient = gradients[panel] - 2.0 * product_total(panel)
        diagonal = pair(panel, panel)
        left = tall(gradient, factor_row(diagonal)).T
        terms[panel, panel] = dot(left, tall(-fz[panel, row], lbar_row(diagonal)))
        if panel == 1:
            terms["inner"] = terms[1, 1] - terms["to_inner"]
        elif panel == 0:
            terms["last"] = terms[0, 0] - terms["to_last"]
        columns[panel] = 0.5 * dot(gradient, head["w" + str(panel)])
        xt_ref[:, panel * NB : (panel + 1) * NB] = columns[panel]
        if panel > 0:
            unit = jnp.where(jnp.logical_and(top, lanes == row * NQ + chip), 1.0, 0.0)
            left = tall(columns[panel], unit).T
            for source in range(panel):
                terms[panel, source] = dot(left, tall(-2.0 * fz[source, row], lbar_row(pair(panel, source))))
        if panel == 1:
            terms["cross"] = terms[1, 0] - terms["to_cross"]

    def diagonal_block(column, inner):
        lower = jnp.where(rows_of > cols_of, inner, jnp.where(rows_of == cols_of, 0.5 * inner, 0.0))
        inverse = head["w" + str(column)]
        return dot(inverse.T, dot(0.5 * (lower + lower.T), inverse))

    def stage(panel):
        if panel == 2:
            found[2, 2] = diagonal_block(2, terms[2, 2])
            bracket[2, 1] = terms[2, 1] - 2.0 * dot(found[2, 2], head["f21"])
            found[2, 1] = 0.5 * dot(bracket[2, 1], head["w1"])
            bracket[2, 0] = terms[2, 0] - 2.0 * (dot(found[2, 1], head["f10"]) + dot(found[2, 2], head["f20"]))
            found[2, 0] = 0.5 * dot(bracket[2, 0], head["w0"])
        elif panel == 1:
            found[1, 1] = diagonal_block(1, terms["inner"])
            bracket[1, 0] = terms["cross"] - 2.0 * dot(found[1, 1], head["f10"])
            found[1, 0] = 0.5 * dot(bracket[1, 0], head["w0"])
        else:
            found[0, 0] = diagonal_block(0, terms["last"])
        for source in range(panel + 1):
            for half in range(2):
                nat[half, pair(panel, source)] = found[panel, source][:, half * HALF : (half + 1) * HALF]
        count = pl.ds(pair(panel, 0), panel + 1)
        copy = remote(nat.at[other, count], nrecv.at[count], xs_sem.at[0, panel], xs_sem.at[1, panel], sibling)
        copy.start()
        pending["xs", panel], pending["xs_out", panel] = copy.wait_recv, copy.wait_send

    def scatter_result(panel):
        landed(("xs", panel))
        first = pair(panel, 0)
        for source in range(panel + 1):
            block = first + source
            for part in range(NQ):
                rows = pl.ds(part, NZ, stride=NQ)
                tsum[part, block] = nat[core, block, rows, :] + nrecv[block, rows, :]
        count = pl.ds(first, panel + 1)
        for index in range(NQ - 1):
            remote(
                tsum.at[plane(index), count], trecv.at[index, count], xx_send.at[panel], xx_recv.at[panel],
                along_col(index),
            ).start()
        later(("xx", panel), trecv.at[:, count], xx_recv.at[panel])
        later(("xx_out", panel), trecv.at[:, count], xx_send.at[panel])

    def result_row(group):
        first, number = (1, 5) if group else (0, 1)
        for panel in (2, 1) if group else (0,):
            landed(("xx", panel))
        count = pl.ds(first, number)
        total = tsum[chip, count]
        for source in range(NQ - 1):
            total = total + trecv[source, count]
        for source in range(number):
            zsend[:, first + source] = total[source].reshape(NZ, 1, HALF)

        def spread(step, carry):
            remote(
                zsend.at[lax.rem(row + step, NZ), count], zrecv.at[step - 1, count],
                xz_send.at[group], xz_recv.at[group], along_row(step),
            ).start()
            return carry

        lax.fori_loop(1, NZ, spread, 0)
        later(("xz", group), zrecv.at[:, count], xz_recv.at[group])
        later(("xz_out", group), zrecv.at[:, count], xz_send.at[group])

    def finish(group):
        landed(("xz", group))
        for block in range(1, 6) if group else (0,):
            total = zsend[row, block]
            for step in range(NZ - 1):
                total = total + zrecv[step, block]
            head_ref[block : block + 1, :] = total

    def carry_over(panel):
        if panel == 2:
            terms["to_inner"] = dot(bracket[2, 1].T, head["f21"])
            terms["to_cross"] = 2.0 * dot(found[2, 1].T, head["f20"])
            terms["to_last"] = dot(bracket[2, 0].T, head["f20"])
        else:
            terms["to_last"] = terms["to_last"] + dot(bracket[1, 0].T, head["f10"])

    phases = [
        (column_gather,), (head_row,), (ring_step, 0), (turn_all,), (ring_step, 1), (column_sibling,), (head_col,),
        (ring_step, 2), (arrange,), (multiply_rows,), (ring_step, 3), (reduce_step, 6),
        (multiply, 1), (reduce_step, 4), (multiply, 0), (scatter_product, 1), (scatter_product, 0), (head_sibling,),
        (reduce_step, 2), (head_arrange,), (start_gradient, 2),
        (trail, 2), (stage, 2), (start_gradient, 1), (carry_over, 2), (scatter_result, 2), (trail, 1), (start_gradient, 0), (stage, 1), (carry_over, 1),
        (trail, 0), (scatter_result, 1), (stage, 0), (scatter_result, 0),
        (result_row, 1), (result_row, 0), (finish, 1), (finish, 0),
    ]
    for phase, *argument in phases:
        phase(*argument)
    later("ring_out", fz.at[pl.ds(0, 2), pl.ds(0, NZ - 1)], ring_send)

    for key in list(pending):
        landed(key)


def scratch():
    f32 = jnp.float32
    dma = pltpu.SemaphoreType.DMA
    return [
        pltpu.VMEM((NZ, 24, 768), f32),
        pltpu.VMEM((24, 768), f32),
        pltpu.VMEM((6, HALF), f32),
        pltpu.VMEM((3, HALF), f32),
        pltpu.VMEM((6, HALF), f32),
        pltpu.VMEM((6, HALF), f32),
        pltpu.VMEM((6, HALF), f32),
        pltpu.VMEM((2, NQ * 24, NZ * 24), f32),
        pltpu.VMEM((3, NZ, 24, NB), f32),
        pltpu.VMEM((2, NQ, 24, NB), f32),
        pltpu.VMEM((NZ, 24, NB), f32),
        pltpu.VMEM((2, REACH, 24, NB), f32),
        pltpu.VMEM((2, 2, NQ, 24, NB), f32),
        pltpu.VMEM((2, NQ, 24, NB), f32),
        pltpu.VMEM((2, NQ - 1, 24, NB), f32),
        pltpu.VMEM((NZ, 6, HALF), f32),
        pltpu.VMEM((2, NQ, 6, NZ, HALF), f32),
        pltpu.VMEM((768, NZ * 24), f32),
        pltpu.VMEM((2, 6, NB, HALF), f32),
        pltpu.VMEM((6, NB, HALF), f32),
        pltpu.VMEM((NQ, 6, NZ, HALF), f32),
        pltpu.VMEM((NQ - 1, 6, NZ, HALF), f32),
        pltpu.VMEM((NZ, 6, 1, HALF), f32),
        pltpu.VMEM((NZ - 1, 6, 1, HALF), f32),
        dma((8,)),
        dma((2,)),
        dma,
        dma((2, 2, REACH)),
        dma,
        dma,
        dma((2,)),
        dma,
        dma((2, REACH)),
        dma,
        dma,
        dma,
        dma,
        dma((2,)),
        dma((2, 2)),
        dma((2,)),
        dma((2,)),
        dma((2, 3)),
        dma((3,)),
        dma((3,)),
        dma((3,)),
        dma((3,)),
    ]


def body(trail_adj, trail_factor, trail_lbar, head_factor, head_inverse, head_lbar):
    return tuple(
        pl.pallas_call(
            kernel,
            out_shape=(
                pltpu.VMEM(trail_lbar.shape, jnp.float32),
                pltpu.VMEM(head_lbar.shape, jnp.float32),
            ),
            in_specs=[pl.BlockSpec(memory_space=pltpu.HBM)] * 6,
            out_specs=(pl.BlockSpec(memory_space=pltpu.VMEM), pl.BlockSpec(memory_space=pltpu.VMEM)),
            scratch_shapes=scratch(),
            compiler_params=pltpu.CompilerParams(
                collective_id=0, has_side_effects=True, vmem_limit_bytes=60 * 1024 * 1024
            ),
            name="chol_adjoint",
        )(trail_adj, trail_factor, trail_lbar, head_factor, head_inverse, head_lbar)
    )


def solution(mesh):
    in_specs = (
        P(None, "col", "row"),
        P(("row", "col"), None),
        P(("row", "col"), None),
        P(None, ("row", "col")),
        P(None, ("row", "col")),
        P(None, ("row", "col")),
    )
    out_specs = (P(("row", "col"), None), P(None, ("row", "col")))
    return jax.shard_map(body, mesh=mesh, in_specs=in_specs, out_specs=out_specs, check_vma=False)
```
